256 devices in a mesh: dp: 8 (over z_hi, x), row: 8 (over y, core), col: 4 (over z_lo).
Axes of the slice: x: 4, y: 4, z: 8 (z_hi: 2, z_lo: 4; z = z_hi * 4 + z_lo), core: 2. Of those that a mesh axis runs over, the one named last changes fastest.
Arguments:
- layer_input: bfloat16 [2048, 4096], P('dp', 'row'), may hold values from -200 to 200
- out_grad: bfloat16 [2048, 4096], P('dp', 'row'), may hold values from -6 to 6
- norm_gain: float32 [4096], P('row'), may hold values from 0.1 to 1.9
- up_weight: bfloat16 [4096, 16384], P('row', 'col'), may hold values from -0.09375 to 0.09375
- down_weight: bfloat16 [16384, 4096], P('col', 'row'), may hold values from -0.046875 to 0.046875
- up_accum: float32 [4096, 16384], P('row', ('col', 'dp')), may hold values from -1131.3708 to 1131.3708
- down_accum: float32 [16384, 4096], P(('col', 'dp'), 'row'), may hold values from -1131.3708 to 1131.3708
- up_rows: float32 [4096], P('row'), may hold values from 307.2 to 3072
- up_cols: float32 [16384], P(('col', 'dp')), may hold values from 307.2 to 3072
- down_rows: float32 [16384], P(('col', 'dp')), may hold values from 307.2 to 3072
- down_cols: float32 [4096], P('row'), may hold values from 307.2 to 3072
Outputs:
- input_grad: bfloat16 [2048, 4096], P('dp', 'row')
- up_update: bfloat16 [4096, 16384], P('row', ('col', 'dp'))
- down_update: bfloat16 [16384, 4096], P(('col', 'dp'), 'row')
- rows_up: float32 [4096], P('row')
- cols_up: float32 [16384], P(('col', 'dp'))
- rows_down: float32 [16384], P(('col', 'dp'))
- cols_down: float32 [4096], P('row')
The draws below stay inside these ranges and needn't reach their ends.
All inputs are finite; a program needn't handle non-finite values.
Results may differ from the reference program's by a relative error of at most 0.013.
Values may be sent and summed in bfloat16 or wider, within the bound.
No kernel may reach another device: no remote copies, remote signals or barrier semaphores. Data moves between devices by JAX's collectives and lax.ppermute only.
A program may use at most 128 MiB of HBM per device.

```python
import math
import jax
import jax.numpy as jnp
from jax import lax

D = 4096
FF = 16384
TOKENS = 2048
N_ROW = 8
N_COL = 4


def draw_layer_input(key, part):
    key = jax.random.fold_in(key, 7)
    entry_key, column_key, row_key = jax.random.split(key, 3)
    entries = jnp.clip(jax.random.normal(entry_key, (TOKENS, D), jnp.float32), -4.0, 4.0)
    growth = jnp.exp(jnp.log(3.0) * jnp.arange(D, dtype=jnp.float32) / D)
    column_scale = growth * jnp.exp(jax.random.uniform(column_key, (D,), jnp.float32, -1.15, 1.15))
    row_scale = 0.25 * jnp.exp(jax.random.uniform(row_key, (TOKENS, 1), jnp.float32, 0.0, 2.3))
    return (entries * column_scale * row_scale).astype(jnp.bfloat16)


def rising_profiles(factor):
    width_rise = jnp.exp(jnp.log(factor) * jnp.arange(D, dtype=jnp.float32) / D)
    block = FF // N_COL
    within = (jnp.arange(FF, dtype=jnp.int32) % block).astype(jnp.float32) / block
    hidden_rise = jnp.exp(jnp.log(factor) * within)
    return (width_rise, hidden_rise)


def accum_entries(key, shape):
    entries = jnp.clip(jax.random.normal(key, shape, jnp.float32), -4.0, 4.0)
    factor = 3.0
    return (entries, factor)


def draw_up_accum(key, part):
    key = jax.random.fold_in(key, 11)
    entries, factor = accum_entries(key, (D, FF))
    width_rise, hidden_rise = rising_profiles(factor)
    return 0.5 * TOKENS ** 0.5 * entries * width_rise[:, None] * hidden_rise[None, :]


def draw_down_accum(key, part):
    key = jax.random.fold_in(key, 13)
    entries, factor = accum_entries(key, (FF, D))
    width_rise, hidden_rise = rising_profiles(factor)
    return 0.5 * TOKENS ** 0.5 * entries * hidden_rise[:, None] * width_rise[None, :]


def shard_levels(key, dims, cuts, smallest, largest):
    gain = 1.0
    for position, blocks in cuts:
        heights = jax.random.uniform(jax.random.fold_in(jax.random.fold_in(key, 6), position), (blocks,), jnp.float32, smallest / len(cuts), largest / len(cuts))
        gain = gain * jnp.repeat(jnp.exp(heights), dims[position] // blocks).reshape((-1,) + (1,) * (len(dims) - 1 - position))
    return gain


def noise(own_key, shape, scale, most, cuts=(), kind=jnp.bfloat16):
    gain = shard_levels(own_key, shape, cuts, -0.22, 0.18) if cuts else 1.0
    values = jax.random.normal(own_key, shape, jnp.float32) * scale * gain
    return jnp.minimum(jnp.maximum(values, -most), most).astype(kind)


def setup_inputs(seed: int = 0) -> dict:
    streams_of = jax.random.split(jax.random.key(seed), 12)
    return {
        "layer_input": draw_layer_input(jax.random.fold_in(streams_of[11], 71), 0),
        "out_grad": noise(streams_of[1], (TOKENS, D), 1.0, 6.0, ((0, 8), (1, 8))),
        "norm_gain": jnp.clip(1.0 + 0.18 * jax.random.normal(streams_of[2], (D,), jnp.float32), 0.1, 1.9),
        "up_weight": noise(streams_of[3], (D, FF), D ** -0.5, 0.09375, ((0, 8), (1, 4))),
        "down_weight": noise(streams_of[4], (FF, D), FF ** -0.5, 0.046875, ((0, 4), (1, 8))),
        "up_accum": draw_up_accum(jax.random.fold_in(streams_of[11], 71), 0),
        "down_accum": draw_down_accum(jax.random.fold_in(streams_of[11], 71), 0),
        "up_rows": jnp.clip(jnp.exp(math.log(3072.0) - 2.3025851 * jax.random.uniform(streams_of[7], (D,), jnp.float32) ** shard_levels(streams_of[7], (D,), ((0, 8),), -0.2, 0.2)), 307.2, 3072.0),
        "up_cols": jnp.clip(jnp.exp(math.log(3072.0) - 2.3025851 * jax.random.uniform(streams_of[8], (FF,), jnp.float32) ** shard_levels(streams_of[8], (FF,), ((0, 32),), -0.2, 0.2)), 307.2, 3072.0),
        "down_rows": jnp.clip(jnp.exp(math.log(3072.0) - 2.3025851 * jax.random.uniform(streams_of[9], (FF,), jnp.float32) ** shard_levels(streams_of[9], (FF,), ((0, 32),), -0.2, 0.2)), 307.2, 3072.0),
        "down_cols": jnp.clip(jnp.exp(math.log(3072.0) - 2.3025851 * jax.random.uniform(streams_of[10], (D,), jnp.float32) ** shard_levels(streams_of[10], (D,), ((0, 8),), -0.2, 0.2)), 307.2, 3072.0),
    }


DECAY_RATE = 0.9
TINY_SQUARE = 1e-30
NORM_EPSILON = 1e-06
GELU_SCALE = 0.7978845608028654
GELU_CUBIC = 0.044715

def gelu_value(operand):
    tangent = jnp.tanh(GELU_SCALE * (operand + GELU_CUBIC * operand * operand * operand))
    return 0.5 * operand * (1.0 + tangent)

def gelu_slope(operand):
    tangent = jnp.tanh(GELU_SCALE * (operand + GELU_CUBIC * operand * operand * operand))
    return 0.5 * (1.0 + tangent) + 0.5 * operand * (1.0 - tangent * tangent) * GELU_SCALE * (1.0 + 3.0 * GELU_CUBIC * operand * operand)

def rounded_blocks(left, right, pieces):
    width = left.shape[1] // pieces
    start_total = jnp.zeros((left.shape[0], right.shape[1]), jnp.float32)

    def add_block(total, index):
        start = (index * width).astype(jnp.int32)
        left_block = lax.dynamic_slice_in_dim(left, start, width, 1)
        right_block = lax.dynamic_slice_in_dim(right, start, width, 0)
        partial_sum = jnp.dot(left_block, right_block, preferred_element_type=jnp.float32)
        partial_sum = lax.optimization_barrier(partial_sum.astype(jnp.bfloat16))
        return (total + partial_sum.astype(jnp.float32), None)
    total, unused = lax.scan(add_block, start_total, jnp.arange(pieces, dtype=jnp.int32))
    return total

def factored_step(grad_total, prior_rows, prior_cols):
    square = grad_total * grad_total
    rows_new = DECAY_RATE * prior_rows + (1.0 - DECAY_RATE) * (lax.optimization_barrier(jnp.mean(square, axis=1)) + TINY_SQUARE)
    cols_new = DECAY_RATE * prior_cols + (1.0 - DECAY_RATE) * (lax.optimization_barrier(jnp.mean(square, axis=0)) + TINY_SQUARE)
    row_level = jnp.mean(rows_new)
    scaled = grad_total * lax.rsqrt(rows_new[:, None] * cols_new[None, :] / row_level)
    return (scaled.astype(jnp.bfloat16), rows_new, cols_new)

def reference(layer_input, out_grad, norm_gain, up_weight, down_weight, up_accum, down_accum, up_rows, up_cols, down_rows, down_cols):
    wide_input = layer_input.astype(jnp.float32)
    inverse = lax.rsqrt(lax.optimization_barrier(jnp.mean(wide_input * wide_input, axis=1, keepdims=True)) + NORM_EPSILON)
    normed = (wide_input * inverse * norm_gain).astype(jnp.bfloat16)
    pre_act = lax.optimization_barrier(rounded_blocks(normed, up_weight, N_ROW).astype(jnp.bfloat16))
    wide_pre = pre_act.astype(jnp.float32)
    activation = gelu_value(wide_pre).astype(jnp.bfloat16)
    slope = gelu_slope(wide_pre)
    act_grad = rounded_blocks(out_grad, down_weight.T, N_ROW)
    hidden_grad = (act_grad * slope).astype(jnp.bfloat16)
    normed_grad = rounded_blocks(hidden_grad, up_weight.T, N_COL)
    gained = normed_grad * norm_gain
    projection = lax.optimization_barrier(jnp.sum(gained * wide_input, axis=1, keepdims=True))
    input_grad = (out_grad.astype(jnp.float32) + inverse * gained - wide_input * inverse * inverse * inverse * projection / D).astype(jnp.bfloat16)
    up_total = up_accum + jnp.dot(normed.T, hidden_grad, preferred_element_type=jnp.float32)
    down_total = down_accum + jnp.dot(activation.T, out_grad, preferred_element_type=jnp.float32)
    up_update, rows_up, cols_up = factored_step(up_total, up_rows, up_cols)
    down_update, rows_down, cols_down = factored_step(down_total, down_rows, down_cols)
    return (input_grad, up_update, down_update, rows_up, cols_up, rows_down, cols_down)
```

```python
import functools

import jax
import jax.numpy as jnp
from jax import lax
from jax.experimental import pallas as pl
from jax.experimental.pallas import tpu as pltpu
from jax.sharding import Mesh
from jax.sharding import PartitionSpec as P

D = 4096
FF = 16384
N_DEVICES = 256

DECAY_RATE = 0.9
TINY_SQUARE = 1e-30
NORM_EPSILON = 1e-06
GELU_SCALE = 0.7978845608028654
GELU_CUBIC = 0.044715

TOK = 256
WIDTH = 512
HID = 4096
HALF = 2048
QUARTER = 64
BLOCK = 512
EXTRA = 128

BF = jnp.bfloat16
F32 = jnp.float32
LAST = (((1,), (1,)), ((), ()))
FIRST = (((0,), (0,)), ((), ()))


def split_parts(column):
    high = column.astype(BF).astype(F32)
    rest = column - high
    middle = rest.astype(BF).astype(F32)
    low = rest - middle
    lane = lax.broadcasted_iota(jnp.int32, (column.shape[0], EXTRA), 1)
    parts = jnp.where(lane == 0, high, jnp.where(lane == 1, middle, jnp.where(lane == 2, low, 0.0)))
    return parts.astype(BF)


def join_parts(block):
    return jnp.sum(block.astype(F32), axis=1, keepdims=True)


def as_column(row):
    return jnp.broadcast_to(row, (128, row.shape[1])).T[:, 0:1]


def whole(shape):
    return pl.BlockSpec(shape, lambda i, s: (0,) * len(shape))


def kernel_call(body, scalars, operands, outs, specs=None, scratch=(), name=None, flops=0):
    specs = specs or {}
    in_specs = [specs.get(i, whole(a.shape)) for i, a in enumerate(operands)]
    out_bytes = sum(s.size * s.dtype.itemsize for s in outs)
    return pl.pallas_call(
        body,
        out_shape=outs,
        grid_spec=pltpu.PrefetchScalarGridSpec(
            num_scalar_prefetch=1,
            grid=(1,),
            in_specs=in_specs,
            out_specs=[whole(s.shape) for s in outs],
            scratch_shapes=list(scratch),
        ),
        compiler_params=pltpu.CompilerParams(vmem_limit_bytes=48 * 1024 * 1024),
        cost_estimate=pl.CostEstimate(flops=flops, bytes_accessed=4 * out_bytes, transcendentals=0),
        name=name,
    )(scalars, *operands)


def shaped(*shape, dtype=BF):
    return jax.ShapeDtypeStruct(shape, dtype)


FORWARD_FLOPS = 2 * TOK * WIDTH * HALF


def pre_other_body(s, li, og, gain, w, lo, sums, out):
    wide = li[...].astype(F32)
    gained = (wide * gain[...]).astype(BF)
    lo[0:TOK, :] = gained
    lo[TOK:, :] = og[...]
    square = jnp.sum(wide * wide, axis=1, keepdims=True)
    sums[...] = jnp.broadcast_to(square, (TOK, 128))
    out[:, 0:HALF] = jnp.dot(gained, w[...], preferred_element_type=F32).astype(BF)
    out[:, HALF:] = split_parts(square)


def pre_own_body(s, lo, sums, w, received, p0, p1, p2, p3, total):
    total[:, 0:HALF] = (
        jnp.dot(lo[0:TOK, :], w[...], preferred_element_type=F32) + received[:, 0:HALF].astype(F32)
    ).astype(BF)
    total[:, HALF:] = split_parts(sums[:, 0:1] + join_parts(received[:, HALF:]))
    for k, piece in enumerate((p0, p1, p2, p3)):
        start = pl.multiple_of(lax.rem(s[1] + k, 4) * QUARTER, QUARTER)
        piece[...] = total[pl.ds(start, QUARTER), :]


def act_other_body(s, og, w, out):
    out[...] = lax.dot_general(og[...], w[...], LAST, preferred_element_type=F32).astype(BF)


def act_own_body(s, og, w, received, p0, p1, p2, p3, total):
    total[...] = (
        lax.dot_general(og[...], w[...], LAST, preferred_element_type=F32) + received[...].astype(F32)
    ).astype(BF)
    for k, piece in enumerate((p0, p1, p2, p3)):
        start = pl.multiple_of(lax.rem(s[1] + k, 4) * QUARTER, QUARTER)
        piece[...] = total[pl.ds(start, QUARTER), :]


def inverse_of(pieces):
    square = sum(join_parts(p[:, HALF:]) for p in pieces)
    return lax.rsqrt(square / D + NORM_EPSILON)


def activation_body(s, p0, p1, p2, p3, a0, a1, a2, a3, scratch):
    pieces = (p0, p1, p2, p3)
    inverse = inverse_of(pieces)
    pre = sum(p[:, 0:HALF].astype(F32) for p in pieces) * inverse
    pre = pre.astype(BF).astype(F32)
    tangent = jnp.tanh(GELU_SCALE * (pre + GELU_CUBIC * pre * pre * pre))
    scratch[...] = (0.5 * pre * (1.0 + tangent)).astype(BF)
    for k, out in enumerate((a0, a1, a2, a3)):
        start = pl.multiple_of(lax.rem(s[2] + k, 4) * BLOCK, BLOCK)
        out[...] = scratch[:, pl.ds(start, BLOCK)]


def hidden_body(s, p0, p1, p2, p3, q0, q1, q2, q3, h0, h1, h2, h3, own):
    pieces = (p0, p1, p2, p3)
    inverse = inverse_of(pieces)
    linear = sum(p[:, 0:HALF].astype(F32) for p in pieces)
    pre = (linear * inverse).astype(BF).astype(F32)
    tangent = jnp.tanh(GELU_SCALE * (pre + GELU_CUBIC * pre * pre * pre))
    slope = 0.5 * (1.0 + tangent) + 0.5 * pre * (1.0 - tangent * tangent) * GELU_SCALE * (
        1.0 + 3.0 * GELU_CUBIC * pre * pre
    )
    act_grad = sum(q[...].astype(F32) for q in (q0, q1, q2, q3))
    hidden = (act_grad * slope * inverse).astype(BF)
    own[:, 0:HALF] = hidden
    projection = jnp.sum(hidden.astype(F32) * linear, axis=1, keepdims=True)
    own[:, HALF:] = split_parts(projection * inverse * inverse / D)
    for k, out in enumerate((h0, h1, h2, h3)):
        start = pl.multiple_of(lax.rem(s[2] + k, 4) * BLOCK, BLOCK)
        out[...] = own[:, pl.ds(start, BLOCK)]


def normed_grad_body(s, mine, other, w, out, hidden):
    c, y = s[0], s[1]
    correction = jnp.zeros((TOK, 1), F32)
    for source, core in ((mine, c), (other, 1 - c)):
        column = pl.multiple_of(core * HALF, HALF)
        for k in range(4):
            row = pl.multiple_of(lax.rem(y - k + 4, 4) * QUARTER, QUARTER)
            block = source[k * QUARTER : (k + 1) * QUARTER, :]
            hidden[pl.ds(row, QUARTER), pl.ds(column, HALF)] = block[:, 0:HALF]
            own = join_parts(block[:, HALF:])
            hidden[pl.ds(row, QUARTER), pl.ds(pl.multiple_of(HID + core * EXTRA, EXTRA), EXTRA)] = split_parts(own)
    correction = join_parts(hidden[:, HID : HID + EXTRA]) + join_parts(hidden[:, HID + EXTRA :])
    out[:, 0:WIDTH] = lax.dot_general(hidden[:, 0:HID], w[...], LAST, preferred_element_type=F32).astype(BF)
    out[:, WIDTH:] = split_parts(correction)


def input_grad_body(s, n0, n1, n2, n3, li, og, gain, out):
    blocks = (n0, n1, n2, n3)
    normed_grad = sum(n[:, 0:WIDTH].astype(F32) for n in blocks)
    correction = sum(join_parts(n[:, WIDTH:]) for n in blocks)
    out[...] = (
        og[...].astype(F32) + gain[...] * normed_grad - li[...].astype(F32) * correction
    ).astype(BF)


def gather_body(s, *refs):
    sources, (inputs, grads) = refs[:8], refs[8:]
    x, h = s[2], s[3]
    for j, source in enumerate(sources):
        group = jnp.where(j < 4, h, 1 - h) * 4 + lax.rem(x - j % 4 + 4, 4)
        start = pl.multiple_of(group * TOK, TOK)
        inputs[pl.ds(start, TOK), :] = source[0:TOK, :]
        grads[pl.ds(start, TOK), :] = source[TOK:, :]


def place_pieces(s, sources, scratch):
    c, y, x = s[0], s[1], s[2]
    for j, source in enumerate(sources):
        h = c if j < 4 else 1 - c
        quarter = lax.rem(y - j % 4 + 4, 4)
        for k in range(4):
            group = h * 4 + lax.rem(x - k + 4, 4)
            start = pl.multiple_of((group * 4 + quarter) * QUARTER, QUARTER)
            scratch[pl.ds(start, QUARTER), :] = source[k * QUARTER : (k + 1) * QUARTER, :]


def down_total_body(s, *refs):
    sources, (grads, accum, total, stats), scratch = refs[:8], refs[8:12], refs[12]
    place_pieces(s, sources, scratch)
    value = accum[...] + lax.dot_general(scratch[...], grads[...], FIRST, preferred_element_type=F32)
    total[...] = value
    square = value * value
    columns = jnp.sum(square, axis=0, keepdims=True)
    stats[0:1, :] = jnp.sum(square.T, axis=0, keepdims=True)
    stats[1:2, :] = columns
    stats[2:3, :] = jnp.broadcast_to(jnp.sum(columns, axis=1, keepdims=True), (1, WIDTH))
    stats[3:, :] = jnp.zeros((5, WIDTH), F32)


def up_total_body(s, *refs):
    sources, (inputs, accum, down_stats, up_rows, down_rows, total, by_row, by_col), scratch = (
        refs[:8],
        refs[8:16],
        refs[16],
    )
    place_pieces(s, sources, scratch)
    value = accum[...] + lax.dot_general(inputs[...], scratch[...], FIRST, preferred_element_type=F32)
    total[...] = value
    square = value * value
    columns = jnp.sum(square, axis=0, keepdims=True)
    everything = jnp.sum(columns, axis=1, keepdims=True)
    up_prior = jnp.sum(up_rows[...], axis=1, keepdims=True)
    down_prior = jnp.sum(down_rows[...], axis=1, keepdims=True)
    up_level = DECAY_RATE * up_prior / 32 + (1.0 - DECAY_RATE) * (everything / FF)
    down_level = DECAY_RATE * down_prior / 8 + (1.0 - DECAY_RATE) * (down_stats[2:3, 0:1] / D)
    by_row[0:1, :] = columns
    by_row[1:2, :] = down_stats[0:1, :]
    by_row[2:3, :] = jnp.broadcast_to(up_level, (1, WIDTH))
    by_row[3:4, :] = jnp.broadcast_to(down_level, (1, WIDTH))
    by_row[4:, :] = jnp.zeros((4, WIDTH), F32)
    by_col[0:1, :] = jnp.sum(square.T, axis=0, keepdims=True)
    by_col[1:2, :] = down_stats[1:2, :]
    by_col[2:, :] = jnp.zeros((6, WIDTH), F32)


def update_body(s, up, down, by_row, by_col, ur, uc, dr, dc, up_out, down_out, ur_out, uc_out, dr_out, dc_out):
    def moment(prior, sums, count):
        return DECAY_RATE * prior + (1.0 - DECAY_RATE) * (sums / count + TINY_SQUARE)

    rows_up = moment(ur[...], by_col[0:1, :], FF)
    cols_up = moment(uc[...], by_row[0:1, :], D)
    rows_down = moment(dr[...], by_row[1:2, :], D)
    cols_down = moment(dc[...], by_col[1:2, :], FF)
    up_level = by_col[2:3, 0:1] / D + (1.0 - DECAY_RATE) * TINY_SQUARE
    down_level = by_col[3:4, 0:1] / FF + (1.0 - DECAY_RATE) * TINY_SQUARE
    ur_out[...], uc_out[...], dr_out[...], dc_out[...] = rows_up, cols_up, rows_down, cols_down
    up_out[...] = (up[...] * lax.rsqrt(as_column(rows_up) * cols_up / up_level)).astype(BF)
    down_out[...] = (down[...] * lax.rsqrt(as_column(rows_down) * cols_down / down_level)).astype(BF)


def shift(value, axis, step, size):
    return lax.ppermute(value, axis, [(i, (i + step) % size) for i in range(size)])


def to_owners(value, step):
    pairs = []
    for h in range(2):
        for x in range(4):
            for c in range(2):
                pairs.append((h * 8 + x * 2 + c, c * 8 + ((x + step) % 4) * 2 + h))
    return lax.ppermute(value, ("zh", "x", "c"), pairs)


def gather_pieces(pieces):
    block = jnp.concatenate([to_owners(p, k) for k, p in enumerate(pieces)], axis=0)
    mine = [block] + [shift(block, "y", k, 4) for k in (1, 2, 3)]
    return mine + [shift(b, "c", 1, 2) for b in mine]


def local(li, og, gain, wu, wd, au, ad, ur, uc, dr, dc):
    scalars = jnp.stack([lax.axis_index("c"), lax.axis_index("y"), lax.axis_index("x"), lax.axis_index("zh")]).astype(
        jnp.int32
    )
    row = lambda v: v.reshape(1, WIDTH)
    gain = row(gain)
    up_half = lambda f: pl.BlockSpec((WIDTH, HALF), lambda i, s: (0, f(s[0])))
    down_half = lambda f: pl.BlockSpec((HALF, WIDTH), lambda i, s: (f(s[0]), 0))
    other, mine = (lambda c: 1 - c), (lambda c: c)

    lo, sums, pre_sent = kernel_call(
        pre_other_body,
        scalars,
        (li, og, gain, wu),
        [shaped(2 * TOK, WIDTH), shaped(TOK, 128, dtype=F32), shaped(TOK, HALF + EXTRA)],
        specs={3: up_half(other)},
        name="pre_other",
        flops=FORWARD_FLOPS,
    )
    pre_received = shift(pre_sent, "c", 1, 2)
    (act_sent,) = kernel_call(
        act_other_body,
        scalars,
        (og, wd),
        [shaped(TOK, HALF)],
        specs={1: down_half(other)},
        name="act_other",
        flops=FORWARD_FLOPS,
    )
    act_received = shift(act_sent, "c", 1, 2)
    pre = kernel_call(
        pre_own_body,
        scalars,
        (lo, sums, wu, pre_received),
        [shaped(QUARTER, HALF + EXTRA)] * 4,
        specs={2: up_half(mine)},
        scratch=[pltpu.VMEM((TOK, HALF + EXTRA), BF)],
        name="pre_own",
        flops=FORWARD_FLOPS,
    )
    pre = [pre[0]] + [shift(pre[k], "y", k, 4) for k in (1, 2, 3)]
    act = kernel_call(
        act_own_body,
        scalars,
        (og, wd, act_received),
        [shaped(QUARTER, HALF)] * 4,
        specs={1: down_half(mine)},
        scratch=[pltpu.VMEM((TOK, HALF), BF)],
        name="act_own",
        flops=FORWARD_FLOPS,
    )
    act = [act[0]] + [shift(act[k], "y", k, 4) for k in (1, 2, 3)]

    lo_other = shift(lo, "zh", 1, 2)
    groups = [lo] + [shift(lo, "x", k, 4) for k in (1, 2, 3)]
    groups += [lo_other] + [shift(lo_other, "x", k, 4) for k in (1, 2, 3)]
    all_inputs, all_grads = kernel_call(
        gather_body, scalars, groups, [shaped(8 * TOK, WIDTH)] * 2, name="gather"
    )

    activation = kernel_call(
        activation_body,
        scalars,
        pre,
        [shaped(QUARTER, BLOCK)] * 4,
        scratch=[pltpu.VMEM((QUARTER, HALF), BF)],
        name="activation",
    )
    *hidden, own = kernel_call(
        hidden_body,
        scalars,
        (*pre, *act),
        [shaped(QUARTER, BLOCK)] * 4 + [shaped(QUARTER, HALF + EXTRA)],
        name="hidden",
    )
    activation = gather_pieces(activation)
    hidden = gather_pieces(hidden)

    own = jnp.concatenate([own] + [shift(own, "y", k, 4) for k in (1, 2, 3)], axis=0)
    own_other = shift(own, "c", 1, 2)
    (partial,) = kernel_call(
        normed_grad_body,
        scalars,
        (own, own_other, wu),
        [shaped(TOK, WIDTH + EXTRA)],
        scratch=[pltpu.VMEM((TOK, HID + 2 * EXTRA), BF)],
        name="normed_grad",
        flops=2 * FORWARD_FLOPS,
    )
    partials = [partial] + [shift(partial, "zl", k, 4) for k in (1, 2, 3)]
    (input_grad,) = kernel_call(
        input_grad_body, scalars, (*partials, li, og, gain), [shaped(TOK, WIDTH)], name="input_grad"
    )

    down_total, down_stats = kernel_call(
        down_total_body,
        scalars,
        (*activation, all_grads, ad),
        [shaped(BLOCK, WIDTH, dtype=F32), shaped(8, WIDTH, dtype=F32)],
        scratch=[pltpu.VMEM((8 * TOK, BLOCK), BF)],
        name="down_total",
        flops=2 * FORWARD_FLOPS,
    )
    up_total, by_row, by_col = kernel_call(
        up_total_body,
        scalars,
        (*hidden, all_inputs, au, down_stats, row(ur), row(dr)),
        [shaped(WIDTH, BLOCK, dtype=F32), shaped(8, WIDTH, dtype=F32), shaped(8, WIDTH, dtype=F32)],
        scratch=[pltpu.VMEM((8 * TOK, BLOCK), BF)],
        name="up_total",
        flops=2 * FORWARD_FLOPS,
    )
    by_row = lax.psum(by_row, ("y", "c"))
    level = (lax.broadcasted_iota(jnp.int32, by_row.shape, 0) & 6) == 2
    by_col = by_col + jnp.where(level, by_row, 0.0)
    for axis in ("x", "zl", "zh"):
        by_col = lax.psum(by_col, axis)
    up_update, down_update, *moments = kernel_call(
        update_body,
        scalars,
        (up_total, down_total, by_row, by_col, row(ur), row(uc), row(dr), row(dc)),
        [shaped(WIDTH, BLOCK), shaped(BLOCK, WIDTH)] + [shaped(1, WIDTH, dtype=F32)] * 4,
        name="update",
    )
    return (input_grad, up_update, down_update, *[m.reshape(WIDTH) for m in moments])


def solution(mesh):
    fine = Mesh(mesh.devices.reshape(2, 4, 4, 2, 4), ("zh", "x", "y", "c", "zl"))
    dp, row, col = ("zh", "x"), ("y", "c"), "zl"
    owner = ("zl", "zh", "x")
    placed = (
        P(dp, row),
        P(dp, row),
        P(row),
        P(row, col),
        P(col, row),
        P(row, owner),
        P(owner, row),
        P(row),
        P(owner),
        P(owner),
        P(row),
    )
    return jax.shard_map(
        local,
        mesh=fine,
        in_specs=placed,
        out_specs=(P(dp, row), P(row, owner), P(owner, row), P(row), P(owner), P(owner), P(row)),
        check_vma=False,
    )
```

```python
import functools

import jax
import jax.numpy as jnp
from jax import lax
from jax.experimental import pallas as pl
from jax.experimental.pallas import tpu as pltpu
from jax.sharding import Mesh
from jax.sharding import PartitionSpec as P

D = 4096
FF = 16384
N_DEVICES = 256

DECAY_RATE = 0.9
TINY_SQUARE = 1e-30
NORM_EPSILON = 1e-06
GELU_SCALE = 0.7978845608028654
GELU_CUBIC = 0.044715

TOK = 256
WIDTH = 512
HID = 4096
HALF = 2048
QUARTER = 64
BLOCK = 512
EXTRA = 128

BF = jnp.bfloat16
F32 = jnp.float32
LAST = (((1,), (1,)), ((), ()))
FIRST = (((0,), (0,)), ((), ()))


def split_parts(column):
    high = column.astype(BF).astype(F32)
    rest = column - high
    middle = rest.astype(BF).astype(F32)
    low = rest - middle
    lane = lax.broadcasted_iota(jnp.int32, (column.shape[0], EXTRA), 1)
    parts = jnp.where(lane == 0, high, jnp.where(lane == 1, middle, jnp.where(lane == 2, low, 0.0)))
    return parts.astype(BF)


def join_parts(block):
    return jnp.sum(block.astype(F32), axis=1, keepdims=True)


def as_column(row):
    return jnp.broadcast_to(row, (128, row.shape[1])).T[:, 0:1]


def whole(shape):
    return pl.BlockSpec(shape, lambda i, s: (0,) * len(shape))


def kernel_call(body, scalars, operands, outs, specs=None, scratch=(), name=None, flops=0, steps=1, limit=24):
    specs = specs or {}
    in_specs = [specs.get(i, whole(a.shape)) for i, a in enumerate(operands)]
    out_bytes = sum(s.size * s.dtype.itemsize for s in outs)
    return pl.pallas_call(
        body,
        out_shape=outs,
        grid_spec=pltpu.PrefetchScalarGridSpec(
            num_scalar_prefetch=1,
            grid=(steps,),
            in_specs=in_specs,
            out_specs=[whole(s.shape) for s in outs],
            scratch_shapes=list(scratch),
        ),
        compiler_params=pltpu.CompilerParams(vmem_limit_bytes=limit * 1024 * 1024),
        cost_estimate=pl.CostEstimate(flops=flops, bytes_accessed=4 * out_bytes, transcendentals=0),
        name=name,
    )(scalars, *operands)


STAY = pl.BlockSpec(memory_space=pltpu.HBM)


def shaped(*shape, dtype=BF):
    return jax.ShapeDtypeStruct(shape, dtype)


FORWARD_FLOPS = 2 * TOK * WIDTH * HALF


STEPS = HALF // BLOCK


def forward_other_body(s, li, og, gain, wu, wd, group, sums, out, wide, factor, sems):
    step = pl.program_id(0)

    @pl.when(step == 0)
    def _():
        copies = [
            pltpu.make_async_copy(li, wide, sems.at[0]),
            pltpu.make_async_copy(gain, factor, sems.at[1]),
            pltpu.make_async_copy(og, group.at[TOK:, :], sems.at[2]),
        ]
        for copy in copies:
            copy.start()
        copies[0].wait()
        copies[1].wait()
        value = wide[...].astype(F32)
        group[0:TOK, :] = (value * factor[...]).astype(BF)
        square = jnp.sum(value * value, axis=1, keepdims=True)
        sums[...] = jnp.broadcast_to(square, (TOK, 128))
        out[:, 2 * HALF :] = split_parts(square)
        copies[2].wait()

    units = pl.ds(pl.multiple_of(step * BLOCK, BLOCK), BLOCK)
    out[:, units] = jnp.dot(group[0:TOK, :], wu[...], preferred_element_type=F32).astype(BF)
    units = pl.ds(pl.multiple_of(HALF + step * BLOCK, BLOCK), BLOCK)
    out[:, units] = lax.dot_general(group[TOK:, :], wd[...], LAST, preferred_element_type=F32).astype(BF)


def forward_own_body(s, group, wu, wd, out):
    step = pl.program_id(0)
    units = pl.ds(pl.multiple_of(step * BLOCK, BLOCK), BLOCK)
    out[:, units] = jnp.dot(group[0:TOK, :], wu[...], preferred_element_type=F32).astype(BF)
    units = pl.ds(pl.multiple_of(HALF + step * BLOCK, BLOCK), BLOCK)
    out[:, units] = lax.dot_general(group[TOK:, :], wd[...], LAST, preferred_element_type=F32).astype(BF)


def forward_sum_body(s, own, sums, received, p0, p1, p2, p3):
    for k, piece in enumerate((p0, p1, p2, p3)):
        rows = pl.ds(pl.multiple_of(lax.rem(s[1] + k, 4) * QUARTER, QUARTER), QUARTER)
        piece[:, 0 : 2 * HALF] = (
            own[rows, :].astype(F32) + received[rows, 0 : 2 * HALF].astype(F32)
        ).astype(BF)
        piece[:, 2 * HALF :] = split_parts(sums[rows, 0:1] + join_parts(received[rows, 2 * HALF :]))


def hidden_body(s, p0, p1, p2, p3, h0, h1, h2, h3, own, scratch):
    pieces = (p0, p1, p2, p3)
    square = sum(join_parts(p[:, 2 * HALF :]) for p in pieces)
    inverse = lax.rsqrt(square / D + NORM_EPSILON)
    linear = sum(p[:, 0:HALF].astype(F32) for p in pieces)
    pre = (linear * inverse).astype(BF).astype(F32)
    tangent = jnp.tanh(GELU_SCALE * (pre + GELU_CUBIC * pre * pre * pre))
    scratch[...] = (0.5 * pre * (1.0 + tangent)).astype(BF)
    slope = 0.5 * (1.0 + tangent) + 0.5 * pre * (1.0 - tangent * tangent) * GELU_SCALE * (
        1.0 + 3.0 * GELU_CUBIC * pre * pre
    )
    act_grad = sum(p[:, HALF : 2 * HALF].astype(F32) for p in pieces)
    hidden = (act_grad * slope * inverse).astype(BF)
    own[:, 0:HALF] = hidden
    projection = jnp.sum(hidden.astype(F32) * linear, axis=1, keepdims=True)
    own[:, HALF:] = split_parts(projection * inverse * inverse / D)
    for k, out in enumerate((h0, h1, h2, h3)):
        units = pl.ds(pl.multiple_of(lax.rem(s[2] + k, 4) * BLOCK, BLOCK), BLOCK)
        out[:, 0:BLOCK] = own[:, units]
        out[:, BLOCK:] = scratch[:, units]


def normed_grad_body(s, mine, other, w, p0, p1, p2, p3, hidden, total):
    c, y = s[0], s[1]
    for source, core in ((mine, c), (other, 1 - c)):
        units = pl.ds(pl.multiple_of(core * HALF, HALF), HALF)
        extra = pl.ds(pl.multiple_of(HID + core * EXTRA, EXTRA), EXTRA)
        for k in range(4):
            rows = pl.ds(pl.multiple_of(lax.rem(y - k + 4, 4) * QUARTER, QUARTER), QUARTER)
            block = source[k * QUARTER : (k + 1) * QUARTER, :]
            hidden[rows, units] = block[:, 0:HALF]
            hidden[rows, extra] = block[:, HALF:]
    total[:, 0:WIDTH] = lax.dot_general(
        hidden[:, 0:HID], w[...], LAST, preferred_element_type=F32
    ).astype(BF)
    total[:, WIDTH:] = split_parts(join_parts(hidden[:, HID:]))
    for k, out in enumerate((p0, p1, p2, p3)):
        out[...] = total[pl.ds(pl.multiple_of(lax.rem(s[4] + k, 4) * QUARTER, QUARTER), QUARTER), :]


def normed_sum_body(s, p0, p1, p2, p3, out):
    pieces = (p0, p1, p2, p3)
    out[:, 0:WIDTH] = sum(p[:, 0:WIDTH].astype(F32) for p in pieces).astype(BF)
    out[:, WIDTH:] = split_parts(sum(join_parts(p[:, WIDTH:]) for p in pieces))


def input_grad_body(s, n0, n1, n2, n3, li, og, gain, out, wide, grads, factor, sems):
    copies = [pltpu.make_async_copy(a, b, sems.at[i]) for i, (a, b) in enumerate(((li, wide), (og, grads), (gain, factor)))]
    for copy in copies:
        copy.start()
    for copy in copies:
        copy.wait()
    for k, piece in enumerate((n0, n1, n2, n3)):
        rows = pl.ds(pl.multiple_of(lax.rem(s[4] - k + 4, 4) * QUARTER, QUARTER), QUARTER)
        normed_grad = piece[:, 0:WIDTH].astype(F32)
        correction = join_parts(piece[:, WIDTH:])
        out[rows, :] = (
            grads[rows, :].astype(F32) + factor[...] * normed_grad - wide[rows, :].astype(F32) * correction
        ).astype(BF)


def place_groups_body(s, own, before, behind, far_inputs, far_grads, inputs, grads):
    def rows(step):
        return pl.ds(pl.multiple_of(lax.rem(s[2] + step, 4) * TOK, TOK), TOK)

    for step, source in ((0, own), (3, before), (1, behind)):
        inputs[rows(step), :] = source[0:TOK, :]
        grads[rows(step), :] = source[TOK:, :]
    inputs[rows(2), :] = far_inputs[...]
    grads[rows(2), :] = far_grads[...]


def place_body(s, b0, b1, b2, b3, out):
    y, x = s[1], s[2]
    for j, source in enumerate((b0, b1, b2, b3)):
        quarter = lax.rem(y - j + 4, 4)
        for k in range(4):
            start = pl.multiple_of((lax.rem(x - k + 4, 4) * 4 + quarter) * QUARTER, QUARTER)
            out[pl.ds(start, QUARTER), :] = source[k * QUARTER : (k + 1) * QUARTER, :]


def grad_of(s, own, other, mine, others, accum, scratch, sem, units_first):
    copy = pltpu.make_async_copy(accum, scratch, sem)
    copy.start()
    value = jnp.zeros((BLOCK, BLOCK), F32)
    for i, source in enumerate((own, other)):
        features = jnp.where(jnp.abs(s[0] - i) == s[3], mine[...], others[...])
        units = source[:, BLOCK:] if units_first else source[:, 0:BLOCK]
        pair = (units, features) if units_first else (features, units)
        value += lax.dot_general(*pair, FIRST, preferred_element_type=F32)
    copy.wait()
    return value + scratch[...]


def down_total_body(s, *refs):
    own, other, group, other_group, accum, total, stats, scratch, sem = refs
    value = grad_of(s, own, other, group, other_group, accum, scratch, sem, True)
    total[...] = value
    square = value * value
    columns = jnp.sum(square, axis=0, keepdims=True)
    stats[0:1, :] = jnp.sum(square.T, axis=0, keepdims=True)
    stats[1:2, :] = columns
    stats[2:3, :] = jnp.broadcast_to(jnp.sum(columns, axis=1, keepdims=True), (1, WIDTH))
    stats[3:, :] = jnp.zeros((5, WIDTH), F32)


def up_total_body(s, *refs):
    own, other, group, other_group, accum, down_stats, up_rows, down_rows, total, by_row, by_col, scratch, sem = refs
    value = grad_of(s, own, other, group, other_group, accum, scratch, sem, False)
    total[...] = value
    square = value * value
    columns = jnp.sum(square, axis=0, keepdims=True)
    everything = jnp.sum(columns, axis=1, keepdims=True)
    up_prior = jnp.sum(up_rows[...], axis=1, keepdims=True)
    down_prior = jnp.sum(down_rows[...], axis=1, keepdims=True)
    up_level = DECAY_RATE * up_prior / 32 + (1.0 - DECAY_RATE) * (everything / FF)
    down_level = DECAY_RATE * down_prior / 8 + (1.0 - DECAY_RATE) * (down_stats[2:3, 0:1] / D)
    by_row[0:1, :] = columns
    by_row[1:2, :] = down_stats[0:1, :]
    by_row[2:3, :] = jnp.broadcast_to(up_level, (1, WIDTH))
    by_row[3:4, :] = jnp.broadcast_to(down_level, (1, WIDTH))
    by_row[4:, :] = jnp.zeros((4, WIDTH), F32)
    by_col[0:1, :] = jnp.sum(square.T, axis=0, keepdims=True)
    by_col[1:2, :] = down_stats[1:2, :]
    by_col[2:, :] = jnp.zeros((6, WIDTH), F32)


def update_body(s, up, down, by_row, by_col, ur, uc, dr, dc, up_out, down_out, ur_out, uc_out, dr_out, dc_out):
    def moment(prior, sums, count):
        return DECAY_RATE * prior + (1.0 - DECAY_RATE) * (sums / count + TINY_SQUARE)

    rows_up = moment(ur[...], by_col[0:1, :], FF)
    cols_up = moment(uc[...], by_row[0:1, :], D)
    rows_down = moment(dr[...], by_row[1:2, :], D)
    cols_down = moment(dc[...], by_col[1:2, :], FF)
    up_level = by_col[2:3, 0:1] / D + (1.0 - DECAY_RATE) * TINY_SQUARE
    down_level = by_col[3:4, 0:1] / FF + (1.0 - DECAY_RATE) * TINY_SQUARE
    ur_out[...], uc_out[...], dr_out[...], dc_out[...] = rows_up, cols_up, rows_down, cols_down
    up_out[...] = (up[...] * lax.rsqrt(as_column(rows_up) * cols_up / up_level)).astype(BF)
    down_out[...] = (down[...] * lax.rsqrt(as_column(rows_down) * cols_down / down_level)).astype(BF)


def shift(value, axis, step, size):
    return lax.ppermute(value, axis, [(i, (i + step) % size) for i in range(size)])


def after(value, *earlier):
    return lax.optimization_barrier((value, *earlier))[0]


def around_x(block):
    return [shift(block, "x", 1, 4), shift(block, "x", 3, 4)]


def far_x(around):
    before, behind = around
    return [*around, shift(before[0:TOK], "x", 1, 4), shift(behind[TOK:], "x", 3, 4)]


def all_x(scalars, block, others, name):
    return kernel_call(
        place_groups_body, scalars, (block, *others), [shaped(4 * TOK, WIDTH)] * 2, name=name
    )


def to_owners(block):
    return lax.ppermute(block, ("zh", "c"), [(0, 0), (1, 2), (2, 1), (3, 3)])


def along_y(block):
    return [block] + [shift(block, "y", k, 4) for k in (1, 2, 3)]


def total_over(value, axis, size):
    return value + sum(shift(value, axis, k, size) for k in range(1, size))


def local(li, og, gain, wu, wd, au, ad, ur, uc, dr, dc):
    scalars = jnp.stack([lax.axis_index("c"), lax.axis_index("y"), lax.axis_index("x"), lax.axis_index("zh"), lax.axis_index("zl")]).astype(
        jnp.int32
    )
    row = lambda v: v.reshape(1, WIDTH)
    gain = row(gain)
    up_half = lambda f: pl.BlockSpec((WIDTH, BLOCK), lambda i, s: (0, f(s[0]) * STEPS + i))
    down_half = lambda f: pl.BlockSpec((BLOCK, WIDTH), lambda i, s: (f(s[0]) * STEPS + i, 0))
    other, mine = (lambda c: 1 - c), (lambda c: c)

    group, sums, sent = kernel_call(
        forward_other_body,
        scalars,
        (li, og, gain, wu, wd),
        [shaped(2 * TOK, WIDTH), shaped(TOK, 128, dtype=F32), shaped(TOK, 2 * HALF + EXTRA)],
        specs={0: STAY, 1: STAY, 2: STAY, 3: up_half(other), 4: down_half(other)},
        scratch=[pltpu.VMEM((TOK, WIDTH), BF), pltpu.VMEM((1, WIDTH), F32), pltpu.SemaphoreType.DMA((3,))],
        name="forward_other",
        flops=2 * FORWARD_FLOPS,
        steps=STEPS,
        limit=48,
    )
    received = shift(sent, "c", 1, 2)
    other_group = shift(group, "zh", 1, 2)
    (own_sums,) = kernel_call(
        forward_own_body,
        scalars,
        (after(group, sent), wu, wd),
        [shaped(TOK, 2 * HALF)],
        specs={1: up_half(mine), 2: down_half(mine)},
        name="forward_own",
        flops=2 * FORWARD_FLOPS,
        steps=STEPS,
        limit=48,
    )
    sums_pieces = kernel_call(
        forward_sum_body,
        scalars,
        (own_sums, sums, received),
        [shaped(QUARTER, 2 * HALF + EXTRA)] * 4,
        name="forward_sum",
    )
    around = far_x(around_x(after(group, sums_pieces[0])))
    sums_pieces = [sums_pieces[0]] + [shift(sums_pieces[k], "y", k, 4) for k in (1, 2, 3)]
    *pieces, own = kernel_call(
        hidden_body,
        scalars,
        (after(sums_pieces[0], *around), *sums_pieces[1:]),
        [shaped(QUARTER, 2 * BLOCK)] * 4 + [shaped(QUARTER, HALF + EXTRA)],
        scratch=[pltpu.VMEM((QUARTER, HALF), BF)],
        name="hidden",
    )
    pieces = [pieces[0]] + [shift(pieces[k], "x", k, 4) for k in (1, 2, 3)]
    units = after(jnp.concatenate(pieces, axis=0), other_group)
    own = along_y(own)
    around_other = [
        shift(after(other_group, units), "x", 1, 4),
        shift(after(other_group, own[1]), "x", 3, 4),
    ]
    units = to_owners(units)
    units = along_y(after(units, around_other[0]))

    own = jnp.concatenate([after(own[0], units[0])] + own[1:], axis=0)
    own_other = after(shift(own, "c", 1, 2), around_other[1])
    partials = kernel_call(
        normed_grad_body,
        scalars,
        (own, own_other, wu),
        [shaped(QUARTER, WIDTH + EXTRA)] * 4,
        scratch=[pltpu.VMEM((TOK, HID + 2 * EXTRA), BF), pltpu.VMEM((TOK, WIDTH + EXTRA), BF)],
        name="normed_grad",
        flops=2 * FORWARD_FLOPS,
    )
    sent = partials
    partials = [partials[0]] + [shift(partials[k], "zl", k, 4) for k in (1, 2, 3)]
    (normed_grad,) = kernel_call(
        normed_sum_body, scalars, partials, [shaped(QUARTER, WIDTH + EXTRA)], name="normed_sum"
    )
    normed_grad = [normed_grad] + [shift(normed_grad, "zl", k, 4) for k in (1, 2, 3)]
    (input_grad,) = kernel_call(
        input_grad_body,
        scalars,
        (*normed_grad, li, og, gain),
        [shaped(TOK, WIDTH)],
        specs={4: STAY, 5: STAY, 6: STAY},
        scratch=[
            pltpu.VMEM((TOK, WIDTH), BF),
            pltpu.VMEM((TOK, WIDTH), BF),
            pltpu.VMEM((1, WIDTH), F32),
            pltpu.SemaphoreType.DMA((3,)),
        ],
        name="input_grad",
    )
    around_other = far_x([after(a, sent[0]) for a in around_other])
    group = all_x(scalars, group, around, "place_inputs")
    other_group = all_x(scalars, other_group, around_other, "place_other_inputs")
    units[0] = after(units[0], normed_grad[0], other_group[0])
    (units,) = kernel_call(place_body, scalars, units, [shaped(4 * TOK, 2 * BLOCK)], name="place")
    units = (units, after(shift(units, "c", 1, 2), input_grad))
    down_total, down_stats = kernel_call(
        down_total_body,
        scalars,
        (*units, group[1], other_group[1], ad),
        [shaped(BLOCK, WIDTH, dtype=F32), shaped(8, WIDTH, dtype=F32)],
        specs={4: STAY},
        scratch=[pltpu.VMEM((BLOCK, WIDTH), F32), pltpu.SemaphoreType.DMA],
        name="down_total",
        flops=2 * FORWARD_FLOPS,
    )
    up_total, by_row, by_col = kernel_call(
        up_total_body,
        scalars,
        (*units, group[0], other_group[0], au, down_stats, row(ur), row(dr)),
        [shaped(WIDTH, BLOCK, dtype=F32), shaped(8, WIDTH, dtype=F32), shaped(8, WIDTH, dtype=F32)],
        specs={4: STAY},
        scratch=[pltpu.VMEM((BLOCK, WIDTH), F32), pltpu.SemaphoreType.DMA],
        name="up_total",
        flops=2 * FORWARD_FLOPS,
    )
    by_row = total_over(total_over(by_row, "c", 2), "y", 4)
    level = (lax.broadcasted_iota(jnp.int32, by_row.shape, 0) & 6) == 2
    by_col = by_col + jnp.where(level, by_row, 0.0)
    by_col = total_over(total_over(total_over(by_col, "x", 4), "zl", 4), "zh", 2)
    up_update, down_update, *moments = kernel_call(
        update_body,
        scalars,
        (up_total, down_total, by_row, by_col, row(ur), row(uc), row(dr), row(dc)),
        [shaped(WIDTH, BLOCK), shaped(BLOCK, WIDTH)] + [shaped(1, WIDTH, dtype=F32)] * 4,
        name="update",
    )
    return (input_grad, up_update, down_update, *[m.reshape(WIDTH) for m in moments])


def solution(mesh):
    fine = Mesh(mesh.devices.reshape(2, 4, 4, 2, 4), ("zh", "x", "y", "c", "zl"))
    dp, row, col = ("zh", "x"), ("y", "c"), "zl"
    owner = ("zl", "zh", "x")
    placed = (
        P(dp, row),
        P(dp, row),
        P(row),
        P(row, col),
        P(col, row),
        P(row, owner),
        P(owner, row),
        P(row),
        P(owner),
        P(owner),
        P(row),
    )
    return jax.shard_map(
        local,
        mesh=fine,
        in_specs=placed,
        out_specs=(P(dp, row), P(row, owner), P(owner, row), P(row), P(owner), P(owner), P(row)),
        check_vma=False,
    )
```

```python
import functools

import jax
import jax.numpy as jnp
from jax import lax
from jax.experimental import pallas as pl
from jax.experimental.pallas import tpu as pltpu
from jax.sharding import Mesh
from jax.sharding import PartitionSpec as P

D = 4096
FF = 16384
N_DEVICES = 256

DECAY_RATE = 0.9
TINY_SQUARE = 1e-30
NORM_EPSILON = 1e-06
GELU_SCALE = 0.7978845608028654
GELU_CUBIC = 0.044715

TOK = 256
WIDTH = 512
HID = 4096
HALF = 2048
QUARTER = 64
BLOCK = 512
EXTRA = 128

BF = jnp.bfloat16
F32 = jnp.float32
LAST = (((1,), (1,)), ((), ()))
FIRST = (((0,), (0,)), ((), ()))


def split_parts(column):
    high = column.astype(BF).astype(F32)
    rest = column - high
    middle = rest.astype(BF).astype(F32)
    low = rest - middle
    lane = lax.broadcasted_iota(jnp.int32, (column.shape[0], EXTRA), 1)
    parts = jnp.where(lane == 0, high, jnp.where(lane == 1, middle, jnp.where(lane == 2, low, 0.0)))
    return parts.astype(BF)


def join_parts(block):
    return jnp.sum(block.astype(F32), axis=1, keepdims=True)


def as_column(row):
    return jnp.broadcast_to(row, (128, row.shape[1])).T[:, 0:1]


def whole(shape):
    return pl.BlockSpec(shape, lambda i, s: (0,) * len(shape))


def kernel_call(body, scalars, operands, outs, specs=None, scratch=(), name=None, flops=0, steps=1, limit=24):
    specs = specs or {}
    in_specs = [specs.get(i, whole(a.shape)) for i, a in enumerate(operands)]
    out_bytes = sum(s.size * s.dtype.itemsize for s in outs)
    return pl.pallas_call(
        body,
        out_shape=outs,
        grid_spec=pltpu.PrefetchScalarGridSpec(
            num_scalar_prefetch=1,
            grid=(steps,),
            in_specs=in_specs,
            out_specs=[whole(s.shape) for s in outs],
            scratch_shapes=list(scratch),
        ),
        compiler_params=pltpu.CompilerParams(vmem_limit_bytes=limit * 1024 * 1024),
        cost_estimate=pl.CostEstimate(flops=flops, bytes_accessed=4 * out_bytes, transcendentals=0),
        name=name,
    )(scalars, *operands)


STAY = pl.BlockSpec(memory_space=pltpu.HBM)


def shaped(*shape, dtype=BF):
    return jax.ShapeDtypeStruct(shape, dtype)


FORWARD_FLOPS = 2 * TOK * WIDTH * HALF


STEPS = HALF // BLOCK


def forward_other_body(s, li, og, gain, wu, wd, group, sums, out, wide, factor, sems):
    step = pl.program_id(0)

    @pl.when(step == 0)
    def _():
        copies = [
            pltpu.make_async_copy(li, wide, sems.at[0]),
            pltpu.make_async_copy(gain, factor, sems.at[1]),
            pltpu.make_async_copy(og, group.at[TOK:, :], sems.at[2]),
        ]
        for copy in copies:
            copy.start()
        copies[0].wait()
        copies[1].wait()
        value = wide[...].astype(F32)
        group[0:TOK, :] = (value * factor[...]).astype(BF)
        square = jnp.sum(value * value, axis=1, keepdims=True)
        sums[...] = jnp.broadcast_to(square, (TOK, 128))
        out[:, 2 * HALF :] = split_parts(square)
        copies[2].wait()

    units = pl.ds(pl.multiple_of(step * BLOCK, BLOCK), BLOCK)
    out[:, units] = jnp.dot(group[0:TOK, :], wu[...], preferred_element_type=F32).astype(BF)
    units = pl.ds(pl.multiple_of(HALF + step * BLOCK, BLOCK), BLOCK)
    out[:, units] = lax.dot_general(group[TOK:, :], wd[...], LAST, preferred_element_type=F32).astype(BF)


def forward_own_body(s, group, wu, wd, out):
    step = pl.program_id(0)
    units = pl.ds(pl.multiple_of(step * BLOCK, BLOCK), BLOCK)
    out[:, units] = jnp.dot(group[0:TOK, :], wu[...], preferred_element_type=F32).astype(BF)
    units = pl.ds(pl.multiple_of(HALF + step * BLOCK, BLOCK), BLOCK)
    out[:, units] = lax.dot_general(group[TOK:, :], wd[...], LAST, preferred_element_type=F32).astype(BF)


def forward_sum_body(s, own, sums, received, p0, p1, p2, p3):
    for k, piece in enumerate((p0, p1, p2, p3)):
        rows = pl.ds(pl.multiple_of(lax.rem(s[1] + k, 4) * QUARTER, QUARTER), QUARTER)
        piece[:, 0 : 2 * HALF] = (
            own[rows, :].astype(F32) + received[rows, 0 : 2 * HALF].astype(F32)
        ).astype(BF)
        piece[:, 2 * HALF :] = split_parts(sums[rows, 0:1] + join_parts(received[rows, 2 * HALF :]))


def hidden_body(s, p0, p1, p2, p3, h0, h1, h2, h3, own, scratch):
    pieces = (p0, p1, p2, p3)
    square = sum(join_parts(p[:, 2 * HALF :]) for p in pieces)
    inverse = lax.rsqrt(square / D + NORM_EPSILON)
    linear = sum(p[:, 0:HALF].astype(F32) for p in pieces)
    pre = (linear * inverse).astype(BF).astype(F32)
    tangent = jnp.tanh(GELU_SCALE * (pre + GELU_CUBIC * pre * pre * pre))
    scratch[...] = (0.5 * pre * (1.0 + tangent)).astype(BF)
    slope = 0.5 * (1.0 + tangent) + 0.5 * pre * (1.0 - tangent * tangent) * GELU_SCALE * (
        1.0 + 3.0 * GELU_CUBIC * pre * pre
    )
    act_grad = sum(p[:, HALF : 2 * HALF].astype(F32) for p in pieces)
    hidden = (act_grad * slope * inverse).astype(BF)
    own[:, 0:HALF] = hidden
    projection = jnp.sum(hidden.astype(F32) * linear, axis=1, keepdims=True)
    own[:, HALF:] = split_parts(projection * inverse * inverse / D)
    for k, out in enumerate((h0, h1, h2, h3)):
        units = pl.ds(pl.multiple_of(lax.rem(s[2] + k, 4) * BLOCK, BLOCK), BLOCK)
        out[:, 0:BLOCK] = own[:, units]
        out[:, BLOCK:] = scratch[:, units]


def normed_grad_body(s, mine, other, w, p0, p1, p2, p3, hidden, total):
    c, y = s[0], s[1]
    for source, core in ((mine, c), (other, 1 - c)):
        units = pl.ds(pl.multiple_of(core * HALF, HALF), HALF)
        extra = pl.ds(pl.multiple_of(HID + core * EXTRA, EXTRA), EXTRA)
        for k in range(4):
            rows = pl.ds(pl.multiple_of(lax.rem(y - k + 4, 4) * QUARTER, QUARTER), QUARTER)
            block = source[k * QUARTER : (k + 1) * QUARTER, :]
            hidden[rows, units] = block[:, 0:HALF]
            hidden[rows, extra] = block[:, HALF:]
    total[:, 0:WIDTH] = lax.dot_general(
        hidden[:, 0:HID], w[...], LAST, preferred_element_type=F32
    ).astype(BF)
    total[:, WIDTH:] = split_parts(join_parts(hidden[:, HID:]))
    for k, out in enumerate((p0, p1, p2, p3)):
        out[...] = total[pl.ds(pl.multiple_of(lax.rem(s[4] + k, 4) * QUARTER, QUARTER), QUARTER), :]


def normed_sum_body(s, p0, p1, p2, p3, out):
    pieces = (p0, p1, p2, p3)
    out[:, 0:WIDTH] = sum(p[:, 0:WIDTH].astype(F32) for p in pieces).astype(BF)
    out[:, WIDTH:] = split_parts(sum(join_parts(p[:, WIDTH:]) for p in pieces))


def input_grad_body(s, n0, n1, n2, n3, li, og, gain, out, wide, grads, factor, sems):
    copies = [pltpu.make_async_copy(a, b, sems.at[i]) for i, (a, b) in enumerate(((li, wide), (og, grads), (gain, factor)))]
    for copy in copies:
        copy.start()
    for copy in copies:
        copy.wait()
    for k, piece in enumerate((n0, n1, n2, n3)):
        rows = pl.ds(pl.multiple_of(lax.rem(s[4] - k + 4, 4) * QUARTER, QUARTER), QUARTER)
        normed_grad = piece[:, 0:WIDTH].astype(F32)
        correction = join_parts(piece[:, WIDTH:])
        out[rows, :] = (
            grads[rows, :].astype(F32) + factor[...] * normed_grad - wide[rows, :].astype(F32) * correction
        ).astype(BF)


def place_groups_body(s, own, before, behind, far_inputs, far_grads, inputs, grads):
    def rows(step):
        return pl.ds(pl.multiple_of(lax.rem(s[2] + step, 4) * TOK, TOK), TOK)

    for step, source in ((0, own), (3, before), (1, behind)):
        inputs[rows(step), :] = source[0:TOK, :]
        grads[rows(step), :] = source[TOK:, :]
    inputs[rows(2), :] = far_inputs[...]
    grads[rows(2), :] = far_grads[...]


def place_body(s, b0, b1, b2, b3, out):
    y, x = s[1], s[2]
    for j, source in enumerate((b0, b1, b2, b3)):
        quarter = lax.rem(y - j + 4, 4)
        for k in range(4):
            start = pl.multiple_of((lax.rem(x - k + 4, 4) * 4 + quarter) * QUARTER, QUARTER)
            out[pl.ds(start, QUARTER), :] = source[k * QUARTER : (k + 1) * QUARTER, :]


def grad_of(s, own, other, mine, others, accum, scratch, sem, units_first):
    copy = pltpu.make_async_copy(accum, scratch, sem)
    copy.start()
    value = jnp.zeros((BLOCK, BLOCK), F32)
    for i, source in enumerate((own, other)):
        features = jnp.where(jnp.abs(s[0] - i) == s[3], mine[...], others[...])
        units = source[:, BLOCK:] if units_first else source[:, 0:BLOCK]
        pair = (units, features) if units_first else (features, units)
        value += lax.dot_general(*pair, FIRST, preferred_element_type=F32)
    copy.wait()
    return value + scratch[...]


def down_total_body(s, *refs):
    own, other, group, other_group, accum, total, stats, scratch, sem = refs
    value = grad_of(s, own, other, group, other_group, accum, scratch, sem, True)
    total[...] = value
    square = value * value
    columns = jnp.sum(square, axis=0, keepdims=True)
    stats[0:1, :] = jnp.sum(square.T, axis=0, keepdims=True)
    stats[1:2, :] = columns
    stats[2:3, :] = jnp.broadcast_to(jnp.sum(columns, axis=1, keepdims=True), (1, WIDTH))
    stats[3:, :] = jnp.zeros((5, WIDTH), F32)


def up_total_body(s, *refs):
    own, other, group, other_group, accum, down_stats, up_rows, down_rows, total, by_row, by_col, scratch, sem = refs
    value = grad_of(s, own, other, group, other_group, accum, scratch, sem, False)
    total[...] = value
    square = value * value
    columns = jnp.sum(square, axis=0, keepdims=True)
    everything = jnp.sum(columns, axis=1, keepdims=True)
    up_prior = jnp.sum(up_rows[...], axis=1, keepdims=True)
    down_prior = jnp.sum(down_rows[...], axis=1, keepdims=True)
    up_level = DECAY_RATE * up_prior / 32 + (1.0 - DECAY_RATE) * (everything / FF)
    down_level = DECAY_RATE * down_prior / 8 + (1.0 - DECAY_RATE) * (down_stats[2:3, 0:1] / D)
    by_row[0:1, :] = columns
    by_row[1:2, :] = down_stats[0:1, :]
    by_row[2:3, :] = jnp.broadcast_to(up_level, (1, WIDTH))
    by_row[3:4, :] = jnp.broadcast_to(down_level, (1, WIDTH))
    by_row[4:, :] = jnp.zeros((4, WIDTH), F32)
    by_col[0:1, :] = jnp.sum(square.T, axis=0, keepdims=True)
    by_col[1:2, :] = down_stats[1:2, :]
    by_col[2:, :] = jnp.zeros((6, WIDTH), F32)


def update_body(s, up, down, by_row, by_col, ur, uc, dr, dc, up_out, down_out, ur_out, uc_out, dr_out, dc_out):
    def moment(prior, sums, count):
        return DECAY_RATE * prior + (1.0 - DECAY_RATE) * (sums / count + TINY_SQUARE)

    rows_up = moment(ur[...], by_col[0:1, :], FF)
    cols_up = moment(uc[...], by_row[0:1, :], D)
    rows_down = moment(dr[...], by_row[1:2, :], D)
    cols_down = moment(dc[...], by_col[1:2, :], FF)
    up_level = by_col[2:3, 0:1] / D + (1.0 - DECAY_RATE) * TINY_SQUARE
    down_level = by_col[3:4, 0:1] / FF + (1.0 - DECAY_RATE) * TINY_SQUARE
    ur_out[...], uc_out[...], dr_out[...], dc_out[...] = rows_up, cols_up, rows_down, cols_down
    up_out[...] = (up[...] * lax.rsqrt(as_column(rows_up) * cols_up / up_level)).astype(BF)
    down_out[...] = (down[...] * lax.rsqrt(as_column(rows_down) * cols_down / down_level)).astype(BF)


def shift(value, axis, step, size):
    return lax.ppermute(value, axis, [(i, (i + step) % size) for i in range(size)])


def after(value, *earlier):
    return lax.optimization_barrier((value, *earlier))[0]


def around_x(block):
    return [shift(block, "x", 1, 4), shift(block, "x", 3, 4)]


def far_x(around):
    before, behind = around
    return [*around, shift(before[0:TOK], "x", 1, 4), shift(behind[TOK:], "x", 3, 4)]


def all_x(scalars, block, others, name):
    return kernel_call(
        place_groups_body, scalars, (block, *others), [shaped(4 * TOK, WIDTH)] * 2, name=name
    )


def to_owners(block):
    return lax.ppermute(block, ("zh", "c"), [(0, 0), (1, 2), (2, 1), (3, 3)])


def along_y(block):
    return [block] + [shift(block, "y", k, 4) for k in (1, 2, 3)]


def total_over(value, axis, size):
    return value + sum(shift(value, axis, k, size) for k in range(1, size))


def local(li, og, gain, wu, wd, au, ad, ur, uc, dr, dc):
    scalars = jnp.stack([lax.axis_index("c"), lax.axis_index("y"), lax.axis_index("x"), lax.axis_index("zh"), lax.axis_index("zl")]).astype(
        jnp.int32
    )
    row = lambda v: v.reshape(1, WIDTH)
    gain = row(gain)
    up_half = lambda f: pl.BlockSpec((WIDTH, BLOCK), lambda i, s: (0, f(s[0]) * STEPS + i))
    down_half = lambda f: pl.BlockSpec((BLOCK, WIDTH), lambda i, s: (f(s[0]) * STEPS + i, 0))
    other, mine = (lambda c: 1 - c), (lambda c: c)

    group, sums, sent = kernel_call(
        forward_other_body,
        scalars,
        (li, og, gain, wu, wd),
        [shaped(2 * TOK, WIDTH), shaped(TOK, 128, dtype=F32), shaped(TOK, 2 * HALF + EXTRA)],
        specs={0: STAY, 1: STAY, 2: STAY, 3: up_half(other), 4: down_half(other)},
        scratch=[pltpu.VMEM((TOK, WIDTH), BF), pltpu.VMEM((1, WIDTH), F32), pltpu.SemaphoreType.DMA((3,))],
        name="forward_other",
        flops=2 * FORWARD_FLOPS,
        steps=STEPS,
        limit=48,
    )
    received = shift(sent, "c", 1, 2)
    other_group = shift(group, "zh", 1, 2)
    (own_sums,) = kernel_call(
        forward_own_body,
        scalars,
        (after(group, sent), wu, wd),
        [shaped(TOK, 2 * HALF)],
        specs={1: up_half(mine), 2: down_half(mine)},
        name="forward_own",
        flops=2 * FORWARD_FLOPS,
        steps=STEPS,
        limit=48,
    )
    sums_pieces = kernel_call(
        forward_sum_body,
        scalars,
        (own_sums, sums, received),
        [shaped(QUARTER, 2 * HALF + EXTRA)] * 4,
        name="forward_sum",
    )
    around = far_x(around_x(after(group, sums_pieces[0])))
    sums_pieces = [sums_pieces[0]] + [shift(sums_pieces[k], "y", k, 4) for k in (1, 2, 3)]
    *pieces, own = kernel_call(
        hidden_body,
        scalars,
        (after(sums_pieces[0], *around), *sums_pieces[1:]),
        [shaped(QUARTER, 2 * BLOCK)] * 4 + [shaped(QUARTER, HALF + EXTRA)],
        scratch=[pltpu.VMEM((QUARTER, HALF), BF)],
        name="hidden",
    )
    pieces = [pieces[0]] + [shift(pieces[k], "x", k, 4) for k in (1, 2, 3)]
    units = after(jnp.concatenate(pieces, axis=0), other_group)
    own = along_y(own)
    around_other = [
        shift(after(other_group, units), "x", 1, 4),
        shift(after(other_group, own[1]), "x", 3, 4),
    ]
    units = to_owners(units)
    units = along_y(after(units, around_other[0]))

    own = jnp.concatenate([after(own[0], units[0])] + own[1:], axis=0)
    own_other = after(shift(own, "c", 1, 2), around_other[1])
    partials = kernel_call(
        normed_grad_body,
        scalars,
        (own, own_other, wu),
        [shaped(QUARTER, WIDTH + EXTRA)] * 4,
        scratch=[pltpu.VMEM((TOK, HID + 2 * EXTRA), BF), pltpu.VMEM((TOK, WIDTH + EXTRA), BF)],
        name="normed_grad",
        flops=2 * FORWARD_FLOPS,
    )
    partials = [partials[0]] + [shift(partials[k], "zl", k, 4) for k in (1, 2, 3)]
    (normed_grad,) = kernel_call(
        normed_sum_body, scalars, partials, [shaped(QUARTER, WIDTH + EXTRA)], name="normed_sum"
    )
    normed_grad = [normed_grad] + [shift(normed_grad, "zl", k, 4) for k in (1, 2, 3)]
    (input_grad,) = kernel_call(
        input_grad_body,
        scalars,
        (*normed_grad, li, og, gain),
        [shaped(TOK, WIDTH)],
        specs={4: STAY, 5: STAY, 6: STAY},
        scratch=[
            pltpu.VMEM((TOK, WIDTH), BF),
            pltpu.VMEM((TOK, WIDTH), BF),
            pltpu.VMEM((1, WIDTH), F32),
            pltpu.SemaphoreType.DMA((3,)),
        ],
        name="input_grad",
    )
    around_other = far_x(around_other)
    group = all_x(scalars, group, around, "place_inputs")
    other_group = all_x(scalars, other_group, around_other, "place_other_inputs")
    units[0] = after(units[0], other_group[0])
    (units,) = kernel_call(place_body, scalars, units, [shaped(4 * TOK, 2 * BLOCK)], name="place")
    units = (units, shift(units, "c", 1, 2))
    down_total, down_stats = kernel_call(
        down_total_body,
        scalars,
        (*units, group[1], other_group[1], ad),
        [shaped(BLOCK, WIDTH, dtype=F32), shaped(8, WIDTH, dtype=F32)],
        specs={4: STAY},
        scratch=[pltpu.VMEM((BLOCK, WIDTH), F32), pltpu.SemaphoreType.DMA],
        name="down_total",
        flops=2 * FORWARD_FLOPS,
    )
    up_total, by_row, by_col = kernel_call(
        up_total_body,
        scalars,
        (*units, group[0], other_group[0], au, down_stats, row(ur), row(dr)),
        [shaped(WIDTH, BLOCK, dtype=F32), shaped(8, WIDTH, dtype=F32), shaped(8, WIDTH, dtype=F32)],
        specs={4: STAY},
        scratch=[pltpu.VMEM((BLOCK, WIDTH), F32), pltpu.SemaphoreType.DMA],
        name="up_total",
        flops=2 * FORWARD_FLOPS,
    )
    by_row = total_over(total_over(by_row, "c", 2), "y", 4)
    level = (lax.broadcasted_iota(jnp.int32, by_row.shape, 0) & 6) == 2
    by_col = by_col + jnp.where(level, by_row, 0.0)
    by_col = total_over(total_over(total_over(by_col, "x", 4), "zl", 4), "zh", 2)
    up_update, down_update, *moments = kernel_call(
        update_body,
        scalars,
        (up_total, down_total, by_row, after(by_col, input_grad), row(ur), row(uc), row(dr), row(dc)),
        [shaped(WIDTH, BLOCK), shaped(BLOCK, WIDTH)] + [shaped(1, WIDTH, dtype=F32)] * 4,
        name="update",
    )
    return (input_grad, up_update, down_update, *[m.reshape(WIDTH) for m in moments])


def solution(mesh):
    fine = Mesh(mesh.devices.reshape(2, 4, 4, 2, 4), ("zh", "x", "y", "c", "zl"))
    dp, row, col = ("zh", "x"), ("y", "c"), "zl"
    owner = ("zl", "zh", "x")
    placed = (
        P(dp, row),
        P(dp, row),
        P(row),
        P(row, col),
        P(col, row),
        P(row, owner),
        P(owner, row),
        P(row),
        P(owner),
        P(owner),
        P(row),
    )
    return jax.shard_map(
        local,
        mesh=fine,
        in_specs=placed,
        out_specs=(P(dp, row), P(row, owner), P(owner, row), P(row), P(owner), P(owner), P(row)),
        check_vma=False,
    )
```
